32 devices in a mesh: rep: 2 (over y), wide: 4 (over z), tp: 4 (over x, core).
Axes of the slice: x: 2, y: 2, z: 4, core: 2. Of those that a mesh axis runs over, the one named last changes fastest.
Arguments:
- tokens: bfloat16 [256, 8192], P(('rep', 'wide'), 'tp'), parts along dimension 0, may hold values from -6 to 6
- adapter_ids: int32 [256], P(('rep', 'wide')), parts along dimension 0, may hold values from 0 to 3, as said below
- adapter_slot: int32 [4], replicated, may hold values from 0 to 3, each once
- gate_weight: bfloat16 [8192, 28672], P('tp', 'wide'), may hold values from -127 to 127
- up_weight: bfloat16 [8192, 28672], P('tp', 'wide'), may hold values from -127 to 127
- hidden_unit_scales: float32 [2, 28672], P(None, 'wide'), may hold values from 7e-05 to 0.0003
- shrink_weight: bfloat16 [4, 8192, 128], P('wide', 'tp'), may hold values from -0.0625 to 0.0625
- expand_weight: bfloat16 [4, 2, 64, 28672], P('tp', None, None, 'wide'), may hold values from -0.75 to 0.75
Outputs:
- hidden: bfloat16 [256, 28672], P(('rep', 'tp'), 'wide'), parts along dimension 0
The draws below stay inside these ranges and needn't reach their ends.
There are 2 independent parts, one for each index of `rep`. The reference program is written for one: setup_inputs(seed, part) draws one part's arguments, and reference() takes and returns one part's arrays. A program takes and returns all parts, laid end to end along the dimension named above; an argument that names none is the same for every part. Nothing has to cross between parts.
Inputs may be any that keep to these rules, and one draw needn't show every extreme that they name: `adapter_ids`: within the rows of one index of wide (aligned blocks of 32 rows) no adapter is named more than 16 times; in every block one adapter, the same one for all blocks of a part, is named exactly 16 times. `adapter_slot`: each slot holds one adapter.
All inputs are finite; a program needn't handle non-finite values.
Results may differ from the reference program's by a relative error of at most 0.015.
Values may be sent and summed in bfloat16 or wider, within the bound.
A program may use at most 192 MiB of HBM per device.

```python
import math
import jax
import jax.numpy as jnp
from jax import lax

D = 8192
HIDDEN_UNITS = 28672
ADAPTER_RANK = 64
ROW_DEV = 32
ADAPTERS = 4
ROWS = 128
CAPACITY = 16
N_WIDE = 4
N_TP = 4


def integer_levels(key):
    return jax.random.randint(key, (D, HIDDEN_UNITS), -127, 128).astype(jnp.float32).astype(jnp.bfloat16)


def draw_gate_weight(key, part):
    key = jax.random.fold_in(key, 3)
    return integer_levels(key)


def draw_up_weight(key, part):
    key = jax.random.fold_in(key, 5)
    return integer_levels(key)


def draw_adapter_ids(key, part):
    key = jax.random.fold_in(key, 11)
    hot_key, block_key = jax.random.split(key)
    hot_adapter = jax.random.randint(hot_key, (), 0, ADAPTERS)

    def one_block(inner_key):
        first_key, second_key = jax.random.split(inner_key)
        ticket_order = jax.random.permutation(first_key, ADAPTERS * CAPACITY)
        owners = (ticket_order // CAPACITY).astype(jnp.int32)
        coldness = (owners != hot_adapter).astype(jnp.int32)
        ranked = owners[jnp.argsort(coldness, stable=True)]
        chosen = ranked[:ROW_DEV]
        return jax.random.permutation(second_key, chosen)
    block_keys = jax.random.split(block_key, N_WIDE)
    return jax.vmap(one_block)(block_keys).reshape(-1).astype(jnp.int32)


def block_scale(key, shape, cuts, least, top_value):
    def one(position, shards_of):
        steps = jax.random.uniform(jax.random.fold_in(jax.random.fold_in(key, 6), position), (shards_of,), jnp.float32, least / len(cuts), top_value / len(cuts))
        return jnp.repeat(jnp.exp(steps), shape[position] // shards_of).reshape((-1,) + (1,) * (len(shape) - position - 1))

    gain = one(*cuts[0])
    for cut in cuts[1:]:
        gain = gain * one(*cut)
    return gain


def scatter_about(stream_key, extent, deviation, bound, pieces=(), held_as=jnp.bfloat16):
    factor_of = block_scale(stream_key, extent, pieces, -0.22, 0.18) if pieces else 1.0
    drawn = jax.random.normal(stream_key, extent, jnp.float32) * deviation * factor_of
    return jnp.minimum(jnp.maximum(drawn, -bound), bound).astype(held_as)


def setup_inputs(seed: int = 0, part: int = 0) -> dict:
    splits = jax.random.split(jax.random.key(seed), 9)
    part_keys = jax.random.split(jax.random.fold_in(splits[8], part), 9)
    tokens = scatter_about(part_keys[0], (ROWS, D), 1.0, 6.0, ((0, 4), (1, 4)))
    adapter_ids = draw_adapter_ids(jax.random.fold_in(jax.random.fold_in(splits[8], part), 71), part)
    adapter_slot = jax.random.permutation(splits[2], ADAPTERS).astype(jnp.int32)
    gate_weight = draw_gate_weight(jax.random.fold_in(splits[8], 71), part)
    up_weight = draw_up_weight(jax.random.fold_in(splits[8], 71), part)
    hidden_unit_scales = jnp.clip(jnp.exp(math.log(0.0003) - 1.45528725 * jax.random.uniform(splits[5], (2, HIDDEN_UNITS), jnp.float32) ** block_scale(splits[5], (2, HIDDEN_UNITS), ((1, 4),), -0.2, 0.2)), 7.000000186963007e-05, 0.0003)
    shrink_weight = scatter_about(splits[6], (ADAPTERS, D, 2 * ADAPTER_RANK), D ** -0.5, 0.0625, ((0, 4), (1, 4)))
    expand_weight = scatter_about(splits[7], (ADAPTERS, 2, ADAPTER_RANK, HIDDEN_UNITS), ADAPTER_RANK ** -0.5, 0.75, ((0, 4), (3, 4)))
    return {"tokens": tokens, "adapter_ids": adapter_ids, "adapter_slot": adapter_slot, "gate_weight": gate_weight, "up_weight": up_weight, "hidden_unit_scales": hidden_unit_scales, "shrink_weight": shrink_weight, "expand_weight": expand_weight}


adapter_gain = 0.5


def reference(tokens, adapter_ids, adapter_slot, gate_weight, up_weight, hidden_unit_scales, shrink_weight, expand_weight):
    slot_of_row = jnp.take(adapter_slot, adapter_ids).astype(jnp.int32)

    def shrink_step(running, slot_number):
        product = jnp.dot(tokens, shrink_weight[slot_number], preferred_element_type=jnp.float32)
        return jnp.where((slot_of_row == slot_number)[:, None], product, running), None

    shrink, _ = lax.scan(shrink_step, jnp.zeros((ROWS, 2 * ADAPTER_RANK), jnp.float32), jnp.arange(ADAPTERS, dtype=jnp.int32))
    shrink = shrink.astype(jnp.bfloat16)
    block_width = D // N_TP
    resident_count = ADAPTERS // N_TP

    def block_step(running, block_index):
        first_feature = (block_index * block_width).astype(jnp.int32)
        first_slot = (block_index * resident_count).astype(jnp.int32)
        token_tile_block = lax.dynamic_slice_in_dim(tokens, first_feature, block_width, 1)
        gate_tile_block = lax.dynamic_slice_in_dim(gate_weight, first_feature, block_width, 0)
        up_tile_block = lax.dynamic_slice_in_dim(up_weight, first_feature, block_width, 0)
        expansion_block = lax.dynamic_slice_in_dim(expand_weight, first_slot, resident_count, 0)
        chosen = (slot_of_row[:, None] == first_slot + jnp.arange(resident_count, dtype=jnp.int32)[None, :]).astype(jnp.bfloat16)
        gate_input_rows = (chosen[:, :, None] * shrink[:, None, :ADAPTER_RANK]).reshape(ROWS, resident_count * ADAPTER_RANK)
        up_input_rows = (chosen[:, :, None] * shrink[:, None, ADAPTER_RANK:]).reshape(ROWS, resident_count * ADAPTER_RANK)
        gate_adapter_term = jnp.dot(token_tile_block, gate_tile_block, preferred_element_type=jnp.float32) * hidden_unit_scales[0] + adapter_gain * jnp.dot(gate_input_rows, expansion_block[:, 0].reshape(resident_count * ADAPTER_RANK, HIDDEN_UNITS), preferred_element_type=jnp.float32)
        up_adapter_term = jnp.dot(token_tile_block, up_tile_block, preferred_element_type=jnp.float32) * hidden_unit_scales[1] + adapter_gain * jnp.dot(up_input_rows, expansion_block[:, 1].reshape(resident_count * ADAPTER_RANK, HIDDEN_UNITS), preferred_element_type=jnp.float32)
        term = jnp.stack([gate_adapter_term, up_adapter_term], axis=1).astype(jnp.bfloat16)
        term = lax.optimization_barrier(term)
        return running + term.astype(jnp.float32), None

    summed, _ = lax.scan(block_step, jnp.zeros((ROWS, 2, HIDDEN_UNITS), jnp.float32), jnp.arange(N_TP, dtype=jnp.int32))
    return (jax.nn.silu(summed[:, 0]) * summed[:, 1]).astype(jnp.bfloat16)
```

```python
import functools

import jax
import jax.numpy as jnp
from jax import lax
from jax.experimental import pallas as pl
from jax.experimental.pallas import tpu as pltpu
from jax.sharding import PartitionSpec as P

adapter_gain = 0.5
lag = 1
weight_bytes = 40 * 2**20
MESH = pl.DeviceIdType.MESH


def fused(
    nw,
    nt,
    bufs,
    tokens,
    slots,
    gate_weight,
    up_weight,
    scales,
    shrink_weight,
    expand_weight,
    out,
    tok_all,
    slot_all,
    wbuf,
    ebuf,
    scale_buf,
    shrink_buf,
    part,
    part_recv,
    low,
    sel,
    term,
    recv1,
    send2,
    recv2,
    w_sem,
    misc_sem,
    tok_send,
    tok_recv,
    part_send_sem,
    part_recv_sem,
    low_send_sem,
    low_recv_sem,
    s1_send,
    s1_recv,
    s2_send,
    s2_recv,
):
    row_dev = tokens.shape[0]
    slots_wide = shrink_weight.shape[0]
    slots_tp = expand_weight.shape[0]
    rank = expand_weight.shape[2]
    sources = slots_tp // slots_wide
    tiles, _, nh, _, row_tp, cb = term.shape
    wide = lax.axis_index("wide")
    tp = lax.axis_index("tp")
    lo = lax.rem(tp, 2)
    hi = lax.div(tp, 2)

    def columns(i):
        return pl.ds(pl.multiple_of(i * cb, cb), cb)

    def weight_copies(i, slot):
        return [
            pltpu.make_async_copy(w.at[:, columns(i)], wbuf.at[slot, p], w_sem.at[slot, p])
            for p, w in enumerate((gate_weight, up_weight))
        ]

    own_rows = pl.ds(pl.multiple_of(wide * row_dev, row_dev), row_dev)
    local = [
        pltpu.make_async_copy(tokens, tok_all.at[own_rows], misc_sem.at[0]),
        pltpu.make_async_copy(slots, slot_all.at[own_rows], misc_sem.at[1]),
        pltpu.make_async_copy(shrink_weight, shrink_buf, misc_sem.at[2]),
        pltpu.make_async_copy(scales, scale_buf, misc_sem.at[3]),
        pltpu.make_async_copy(expand_weight, ebuf, misc_sem.at[4]),
    ]

    barrier = pltpu.get_barrier_semaphore()
    for d in range(1, nw):
        pl.semaphore_signal(
            barrier, inc=1, device_id={"wide": lax.rem(wide + d, nw)}, device_id_type=MESH
        )
    for d in range(1, nt):
        pl.semaphore_signal(
            barrier, inc=1, device_id={"tp": lax.rem(tp + d, nt)}, device_id_type=MESH
        )
    for copy in local:
        copy.start()
    for i in range(bufs):
        for copy in weight_copies(i, i):
            copy.start()
    pl.semaphore_wait(barrier, nw + nt - 2)

    def token_copies(d):
        there = {"wide": lax.rem(wide + d, nw)}
        return [
            pltpu.make_async_remote_copy(
                src_ref=src,
                dst_ref=dst.at[own_rows],
                send_sem=tok_send.at[d - 1, k],
                recv_sem=tok_recv.at[d - 1, k],
                device_id=there,
                device_id_type=MESH,
            )
            for k, (src, dst) in enumerate(((tokens, tok_all), (slots, slot_all)))
        ]

    gather = [token_copies(d) for d in range(1, nw)]
    for pair in gather:
        for copy in pair:
            copy.start()
    for copy in local:
        copy.wait()
    for pair in gather:
        for copy in pair:
            copy.wait()

    total = None
    for j in range(slots_wide):
        product = jnp.dot(tok_all[...], shrink_buf[j], preferred_element_type=jnp.float32)
        product = jnp.where(slot_all[...] == wide * slots_wide + j, product, 0.0)
        total = product if total is None else total + product
    part[...] = total

    owner = lax.div(wide, sources)
    ahead = lax.rem(owner - tp + nt, nt)

    def part_copy(d):
        return pltpu.make_async_remote_copy(
            src_ref=part,
            dst_ref=part_recv.at[d - 1],
            send_sem=part_send_sem,
            recv_sem=part_recv_sem.at[d - 1],
            device_id={"tp": owner},
            device_id_type=MESH,
        )

    for d in range(1, nt):

        @pl.when(ahead == d)
        def _():
            part_copy(d).start()

    def low_copy(d, j):
        return pltpu.make_async_remote_copy(
            src_ref=low.at[j],
            dst_ref=low.at[j],
            send_sem=low_send_sem.at[d - 1],
            recv_sem=low_recv_sem.at[j],
            device_id={"wide": lax.rem(wide + d, nw)},
            device_id_type=MESH,
        )

    own_source = lax.rem(wide, sources)

    @pl.when(ahead == 0)
    def _():
        value = part[...]
        for d in range(1, nt):
            part_copy(d).wait_recv()
            value = value + part_recv[d - 1]
        low[own_source] = value.astype(jnp.bfloat16)
        for d in range(1, nw):
            low_copy(d, own_source).start()

    for j in range(sources):

        @pl.when(wide != tp * sources + j)
        def _():
            low_copy(1, j).wait_recv()

    for j in range(slots_tp):
        chosen = jnp.where(
            slot_all[...] == tp * slots_tp + j, low[j // slots_wide].astype(jnp.float32), 0.0
        ).astype(jnp.bfloat16)
        for p in range(2):
            sel[p, :, j * rank : (j + 1) * rank] = chosen[:, p * rank : (p + 1) * rank]

    for d in range(1, nt):

        @pl.when(ahead == d)
        def _():
            part_copy(d).wait_send()

    @pl.when(ahead == 0)
    def _():
        for d in range(1, nw):
            low_copy(d, own_source).wait_send()

    def first_copy(i):
        return pltpu.make_async_remote_copy(
            src_ref=term.at[i, 1 - lo],
            dst_ref=recv1.at[i],
            send_sem=s1_send.at[i],
            recv_sem=s1_recv.at[i],
            device_id={"tp": 2 * hi + 1 - lo},
            device_id_type=MESH,
        )

    def second_copy(i, d):
        return pltpu.make_async_remote_copy(
            src_ref=send2.at[i, d - 1],
            dst_ref=recv2.at[i, d - 1],
            send_sem=s2_send.at[i, d - 1],
            recv_sem=s2_recv.at[i, d - 1],
            device_id={"tp": 2 * lax.rem(hi + d, nh) + lo},
            device_id_type=MESH,
        )

    def exchange(i):
        first_copy(i).wait_recv()
        for d in range(1, nh):
            h = lax.rem(hi + d, nh)
            send2[i, d - 1] = (
                term[i, lo, h].astype(jnp.float32) + recv1[i, h].astype(jnp.float32)
            ).astype(jnp.bfloat16)
            second_copy(i, d).start()

    def tile(i, carry):
        slot = lax.rem(i, bufs)
        for copy in weight_copies(i, slot):
            copy.wait()
        for p in range(2):
            main = jnp.dot(tok_all[...], wbuf[slot, p], preferred_element_type=jnp.float32)
            e = ebuf[:, p, :, columns(i)].reshape(slots_tp * rank, cb)
            low_term = jnp.dot(sel[p], e, preferred_element_type=jnp.float32)
            value = main * scale_buf[pl.ds(p, 1), columns(i)] + adapter_gain * low_term
            value = value.astype(jnp.bfloat16)
            for t in range(nt):
                term[i, t % 2, t // 2, p] = value[t * row_tp : (t + 1) * row_tp]
        first_copy(i).start()

        @pl.when(i + bufs < tiles)
        def _():
            for copy in weight_copies(i + bufs, slot):
                copy.start()

        @pl.when(i >= lag)
        def _():
            exchange(i - lag)

        return carry

    lax.fori_loop(0, tiles, tile, 0)
    for i in range(max(tiles - lag, 0), tiles):
        exchange(i)

    def finish(i, carry):
        sums = []
        for d in range(1, nh):
            second_copy(i, d).wait_recv()
        for p in range(2):
            value = term[i, lo, hi, p].astype(jnp.float32) + recv1[i, hi, p].astype(jnp.float32)
            for d in range(1, nh):
                value = value + recv2[i, d - 1, p].astype(jnp.float32)
            sums.append(value)
        gate, up = sums
        out[:, columns(i)] = (gate / (1.0 + jnp.exp(-gate)) * up).astype(jnp.bfloat16)
        return carry

    lax.fori_loop(0, tiles, finish, 0)

    def drain(i, carry):
        first_copy(i).wait_send()
        for d in range(1, nh):
            second_copy(i, d).wait_send()
        return carry

    lax.fori_loop(0, tiles, drain, 0)


def shards(
    nw,
    nt,
    tokens,
    adapter_ids,
    adapter_slot,
    gate_weight,
    up_weight,
    hidden_unit_scales,
    shrink_weight,
    expand_weight,
):
    row_dev, features = tokens.shape
    columns = gate_weight.shape[1]
    rows = row_dev * nw
    row_tp = rows // nt
    nh = nt // 2
    slots_tp, _, rank, _ = expand_weight.shape
    slots_wide = shrink_weight.shape[0]
    sources = slots_tp // slots_wide
    cb = max(c for c in (128, 256, 512) if columns % c == 0)
    tiles = columns // cb
    bufs = max(1, min(tiles, weight_bytes // (features * cb * 4)))

    matches = adapter_ids[:, None] == jnp.arange(adapter_slot.shape[0], dtype=jnp.int32)[None, :]
    slot = jnp.sum(jnp.where(matches, adapter_slot[None, :], 0), axis=1)
    slots = jnp.broadcast_to(slot[:, None], (row_dev, 2 * rank))

    bf16, f32 = jnp.bfloat16, jnp.float32
    DMA = pltpu.SemaphoreType.DMA
    return pl.pallas_call(
        functools.partial(fused, nw, nt, bufs),
        out_shape=jax.ShapeDtypeStruct((row_tp, columns), bf16),
        in_specs=[pl.BlockSpec(memory_space=pl.ANY)] * 7,
        out_specs=pl.BlockSpec(memory_space=pltpu.VMEM),
        scratch_shapes=[
            pltpu.VMEM((rows, features), bf16),
            pltpu.VMEM((rows, 2 * rank), jnp.int32),
            pltpu.VMEM((bufs, 2, features, cb), bf16),
            pltpu.VMEM(expand_weight.shape, bf16),
            pltpu.VMEM((2, columns), f32),
            pltpu.VMEM(shrink_weight.shape, bf16),
            pltpu.VMEM((rows, 2 * rank), f32),
            pltpu.VMEM((nt - 1, rows, 2 * rank), f32),
            pltpu.VMEM((sources, rows, 2 * rank), bf16),
            pltpu.VMEM((2, rows, slots_tp * rank), bf16),
            pltpu.VMEM((tiles, 2, nh, 2, row_tp, cb), bf16),
            pltpu.VMEM((tiles, nh, 2, row_tp, cb), bf16),
            pltpu.VMEM((tiles, nh - 1, 2, row_tp, cb), bf16),
            pltpu.VMEM((tiles, nh - 1, 2, row_tp, cb), bf16),
            DMA((bufs, 2)),
            DMA((5,)),
            DMA((nw - 1, 2)),
            DMA((nw - 1, 2)),
            DMA,
            DMA((nt - 1,)),
            DMA((nw - 1,)),
            DMA((sources,)),
            DMA((tiles,)),
            DMA((tiles,)),
            DMA((tiles, nh - 1)),
            DMA((tiles, nh - 1)),
        ],
        compiler_params=pltpu.CompilerParams(
            collective_id=0, has_side_effects=True, vmem_limit_bytes=60 * 2**20
        ),
        cost_estimate=pl.CostEstimate(
            flops=4 * rows * features * columns,
            bytes_accessed=4 * features * columns,
            transcendentals=row_tp * columns,
        ),
    )(
        tokens,
        slots,
        gate_weight,
        up_weight,
        hidden_unit_scales,
        shrink_weight,
        expand_weight,
    )


def solution(mesh):
    return jax.shard_map(
        functools.partial(shards, mesh.shape["wide"], mesh.shape["tp"]),
        mesh=mesh,
        in_specs=(
            P(("rep", "wide"), "tp"),
            P(("rep", "wide")),
            P(),
            P("tp", "wide"),
            P("tp", "wide"),
            P(None, "wide"),
            P("wide", "tp", None),
            P("tp", None, None, "wide"),
        ),
        out_specs=P(("rep", "tp"), "wide"),
        check_vma=False,
    )
```

```python
import functools

import jax
import jax.numpy as jnp
from jax import lax
from jax.experimental import pallas as pl
from jax.experimental.pallas import tpu as pltpu
from jax.sharding import PartitionSpec as P

adapter_gain = 0.5
lag = 1
early = 3
weight_bytes = 40 * 2**20
MESH = pl.DeviceIdType.MESH


def fused(
    nw,
    nt,
    bufs,
    tokens,
    ids,
    table,
    gate_weight,
    up_weight,
    scales,
    shrink_weight,
    expand_weight,
    out,
    tok_all,
    slot_own,
    slot_rows,
    slot_all,
    wbuf,
    ebuf,
    scale_buf,
    shrink_buf,
    part,
    part_recv,
    low,
    sel,
    acc,
    term,
    recv1,
    send2,
    recv2,
    w_sem,
    misc_sem,
    tok_send,
    tok_recv,
    slot_send,
    slot_recv,
    part_send_sem,
    part_recv_sem,
    low_send_sem,
    low_recv_sem,
    s1_send,
    s1_recv,
    s2_send,
    s2_recv,
):
    row_dev = tokens.shape[0]
    slots_wide = shrink_weight.shape[0]
    slots_tp = expand_weight.shape[0]
    rank = expand_weight.shape[2]
    sources = slots_tp // slots_wide
    tiles, _, nh, _, row_tp, cb = term.shape
    wide = lax.axis_index("wide")
    tp = lax.axis_index("tp")
    lo = lax.rem(tp, 2)
    hi = lax.div(tp, 2)

    def columns(i):
        return pl.ds(pl.multiple_of(i * cb, cb), cb)

    def weight_copies(i, slot):
        return [
            pltpu.make_async_copy(w.at[:, columns(i)], wbuf.at[slot, p], w_sem.at[slot, p])
            for p, w in enumerate((gate_weight, up_weight))
        ]

    own_rows = pl.ds(pl.multiple_of(wide * row_dev, row_dev), row_dev)
    local = [
        pltpu.make_async_copy(tokens, tok_all.at[own_rows], misc_sem.at[0]),
        pltpu.make_async_copy(shrink_weight, shrink_buf, misc_sem.at[1]),
        pltpu.make_async_copy(scales, scale_buf, misc_sem.at[2]),
        pltpu.make_async_copy(expand_weight, ebuf, misc_sem.at[3]),
    ]

    barrier = pltpu.get_barrier_semaphore()
    for d in range(1, nw):
        pl.semaphore_signal(
            barrier, inc=1, device_id={"wide": lax.rem(wide + d, nw)}, device_id_type=MESH
        )
    for d in range(1, nt):
        pl.semaphore_signal(
            barrier, inc=1, device_id={"tp": lax.rem(tp + d, nt)}, device_id_type=MESH
        )
    for copy in local:
        copy.start()
    for i in range(bufs):
        for copy in weight_copies(i, i):
            copy.start()
    pl.semaphore_wait(barrier, nw + nt - 2)

    def token_copy(d):
        return pltpu.make_async_remote_copy(
            src_ref=tokens,
            dst_ref=tok_all.at[own_rows],
            send_sem=tok_send.at[d - 1],
            recv_sem=tok_recv.at[d - 1],
            device_id={"wide": lax.rem(wide + d, nw)},
            device_id_type=MESH,
        )

    slot_row = jnp.zeros(ids.shape, jnp.float32)
    for a in range(table.shape[1]):
        slot_row = jnp.where(ids[...] == a, table[0, a].astype(jnp.float32), slot_row)
    slot_own[...] = jnp.zeros_like(slot_own)
    slot_own[0:1, 0:row_dev] = slot_row
    slot_rows[wide] = slot_own[...]

    def slot_copy(d):
        return pltpu.make_async_remote_copy(
            src_ref=slot_own,
            dst_ref=slot_rows.at[wide],
            send_sem=slot_send.at[d - 1],
            recv_sem=slot_recv.at[d - 1],
            device_id={"wide": lax.rem(wide + d, nw)},
            device_id_type=MESH,
        )

    for d in range(1, nw):
        slot_copy(d).start()

    for d in range(1, nw):
        token_copy(d).start()
    for copy in local:
        copy.wait()
    for d in range(1, nw):
        slot_copy(d).wait()
    diagonal = lax.broadcasted_iota(jnp.int32, (row_dev, row_dev), 0) == lax.broadcasted_iota(
        jnp.int32, (row_dev, row_dev), 1
    )
    for b in range(nw):
        row = jnp.broadcast_to(slot_rows[b, 0:1, 0:row_dev], (row_dev, row_dev))
        column = jnp.sum(jnp.where(diagonal, row, 0.0), axis=1, keepdims=True)
        slot_all[b * row_dev : (b + 1) * row_dev, :] = jnp.broadcast_to(
            column, (row_dev, slot_all.shape[1])
        )

    owner = lax.div(wide, sources)
    ahead = lax.rem(owner - tp + nt, nt)

    def part_copy(d):
        return pltpu.make_async_remote_copy(
            src_ref=part,
            dst_ref=part_recv.at[d - 1],
            send_sem=part_send_sem,
            recv_sem=part_recv_sem.at[d - 1],
            device_id={"tp": owner},
            device_id_type=MESH,
        )

    for d in range(1, nw):
        token_copy(d).wait()

    total = None
    for j in range(slots_wide):
        product = jnp.dot(tok_all[...], shrink_buf[j], preferred_element_type=jnp.float32)
        mine = slot_all[...] == (wide * slots_wide + j).astype(jnp.float32)
        product = jnp.where(mine, product, 0.0)
        total = product if total is None else total + product
    part[...] = total
    for d in range(1, nt):

        @pl.when(ahead == d)
        def _():
            part_copy(d).start()

    def low_copy(d, j):
        return pltpu.make_async_remote_copy(
            src_ref=low.at[j],
            dst_ref=low.at[j],
            send_sem=low_send_sem.at[d - 1],
            recv_sem=low_recv_sem.at[j],
            device_id={"wide": lax.rem(wide + d, nw)},
            device_id_type=MESH,
        )

    own_source = lax.rem(wide, sources)

    @pl.when(ahead == 0)
    def _():
        value = part[...]
        for d in range(1, nt):
            part_copy(d).wait_recv()
            value = value + part_recv[d - 1]
        low[own_source] = value.astype(jnp.bfloat16)
        for d in range(1, nw):
            low_copy(d, own_source).start()

    def main_term(i, p):
        main = jnp.dot(
            tok_all[...], wbuf[lax.rem(i, bufs), p], preferred_element_type=jnp.float32
        )
        return main * scale_buf[pl.ds(p, 1), columns(i)]

    def begin(i, carry):
        for p, copy in enumerate(weight_copies(i, lax.rem(i, bufs))):
            copy.wait()
            acc[i, p] = main_term(i, p)

        @pl.when(i + bufs < tiles)
        def _():
            for copy in weight_copies(i + bufs, lax.rem(i, bufs)):
                copy.start()

        return carry

    ahead_tiles = acc.shape[0]
    lax.fori_loop(0, ahead_tiles, begin, 0)

    for j in range(sources):

        @pl.when(wide != tp * sources + j)
        def _():
            low_copy(1, j).wait_recv()

    for j in range(slots_tp):
        chosen = jnp.where(
            slot_all[...] == (tp * slots_tp + j).astype(jnp.float32), low[j // slots_wide].astype(jnp.float32), 0.0
        ).astype(jnp.bfloat16)
        for p in range(2):
            sel[p, :, j * rank : (j + 1) * rank] = chosen[:, p * rank : (p + 1) * rank]

    for d in range(1, nt):

        @pl.when(ahead == d)
        def _():
            part_copy(d).wait_send()

    @pl.when(ahead == 0)
    def _():
        for d in range(1, nw):
            low_copy(d, own_source).wait_send()

    def first_copy(i):
        return pltpu.make_async_remote_copy(
            src_ref=term.at[i, 1 - lo],
            dst_ref=recv1.at[i],
            send_sem=s1_send.at[i],
            recv_sem=s1_recv.at[i],
            device_id={"tp": 2 * hi + 1 - lo},
            device_id_type=MESH,
        )

    def second_copy(i, d):
        return pltpu.make_async_remote_copy(
            src_ref=send2.at[i, d - 1],
            dst_ref=recv2.at[i, d - 1],
            send_sem=s2_send.at[i, d - 1],
            recv_sem=s2_recv.at[i, d - 1],
            device_id={"tp": 2 * lax.rem(hi + d, nh) + lo},
            device_id_type=MESH,
        )

    def exchange(i):
        first_copy(i).wait_recv()
        for d in range(1, nh):
            h = lax.rem(hi + d, nh)
            send2[i, d - 1] = (
                term[i, lo, h].astype(jnp.float32) + recv1[i, h].astype(jnp.float32)
            ).astype(jnp.bfloat16)
            second_copy(i, d).start()

    def send_term(i, p, main):
        e = ebuf[:, p, :, columns(i)].reshape(slots_tp * rank, cb)
        low_term = jnp.dot(sel[p], e, preferred_element_type=jnp.float32)
        value = (main + adapter_gain * low_term).astype(jnp.bfloat16)
        for t in range(nt):
            term[i, t % 2, t // 2, p] = value[t * row_tp : (t + 1) * row_tp]

    def complete(i, carry):
        for p in range(2):
            send_term(i, p, acc[i, p])
        first_copy(i).start()

        @pl.when(i >= lag)
        def _():
            exchange(i - lag)

        return carry

    lax.fori_loop(0, ahead_tiles, complete, 0)

    def tile(i, carry):
        slot = lax.rem(i, bufs)
        for p, copy in enumerate(weight_copies(i, slot)):
            copy.wait()
            send_term(i, p, main_term(i, p))
        first_copy(i).start()

        @pl.when(i + bufs < tiles)
        def _():
            for copy in weight_copies(i + bufs, slot):
                copy.start()

        exchange(i - lag)
        return carry

    lax.fori_loop(ahead_tiles, tiles, tile, 0)
    for i in range(max(tiles - lag, 0), tiles):
        exchange(i)

    def finish(i, carry):
        sums = []
        for d in range(1, nh):
            second_copy(i, d).wait_recv()
        for p in range(2):
            value = term[i, lo, hi, p].astype(jnp.float32) + recv1[i, hi, p].astype(jnp.float32)
            for d in range(1, nh):
                value = value + recv2[i, d - 1, p].astype(jnp.float32)
            sums.append(value)
        gate, up = sums
        out[:, columns(i)] = (gate / (1.0 + jnp.exp(-gate)) * up).astype(jnp.bfloat16)
        return carry

    lax.fori_loop(0, tiles, finish, 0)

    def drain(i, carry):
        first_copy(i).wait_send()
        for d in range(1, nh):
            second_copy(i, d).wait_send()
        return carry

    lax.fori_loop(0, tiles, drain, 0)


def shards(
    nw,
    nt,
    tokens,
    adapter_ids,
    adapter_slot,
    gate_weight,
    up_weight,
    hidden_unit_scales,
    shrink_weight,
    expand_weight,
):
    row_dev, features = tokens.shape
    columns = gate_weight.shape[1]
    rows = row_dev * nw
    row_tp = rows // nt
    nh = nt // 2
    slots_tp, _, rank, _ = expand_weight.shape
    slots_wide = shrink_weight.shape[0]
    sources = slots_tp // slots_wide
    cb = max(c for c in (128, 256, 512) if columns % c == 0)
    tiles = columns // cb
    bufs = max(1, min(tiles, weight_bytes // (features * cb * 4)))

    ahead_tiles = max(lag, min(early, bufs, tiles))
    slot_lanes = -(-row_dev // 128) * 128
    bf16, f32 = jnp.bfloat16, jnp.float32
    DMA = pltpu.SemaphoreType.DMA
    return pl.pallas_call(
        functools.partial(fused, nw, nt, bufs),
        out_shape=jax.ShapeDtypeStruct((row_tp, columns), bf16),
        in_specs=[
            pl.BlockSpec(memory_space=pl.ANY),
            pl.BlockSpec(memory_space=pltpu.VMEM),
            pl.BlockSpec(memory_space=pltpu.SMEM),
        ]
        + [pl.BlockSpec(memory_space=pl.ANY)] * 5,
        out_specs=pl.BlockSpec(memory_space=pltpu.VMEM),
        scratch_shapes=[
            pltpu.VMEM((rows, features), bf16),
            pltpu.VMEM((8, slot_lanes), f32),
            pltpu.VMEM((nw, 8, slot_lanes), f32),
            pltpu.VMEM((rows, 2 * rank), f32),
            pltpu.VMEM((bufs, 2, features, cb), bf16),
            pltpu.VMEM(expand_weight.shape, bf16),
            pltpu.VMEM((2, columns), f32),
            pltpu.VMEM(shrink_weight.shape, bf16),
            pltpu.VMEM((rows, 2 * rank), f32),
            pltpu.VMEM((nt - 1, rows, 2 * rank), f32),
            pltpu.VMEM((sources, rows, 2 * rank), bf16),
            pltpu.VMEM((2, rows, slots_tp * rank), bf16),
            pltpu.VMEM((ahead_tiles, 2, rows, cb), f32),
            pltpu.VMEM((tiles, 2, nh, 2, row_tp, cb), bf16),
            pltpu.VMEM((tiles, nh, 2, row_tp, cb), bf16),
            pltpu.VMEM((tiles, nh - 1, 2, row_tp, cb), bf16),
            pltpu.VMEM((tiles, nh - 1, 2, row_tp, cb), bf16),
            DMA((bufs, 2)),
            DMA((4,)),
            DMA((nw - 1,)),
            DMA((nw - 1,)),
            DMA((nw - 1,)),
            DMA((nw - 1,)),
            DMA,
            DMA((nt - 1,)),
            DMA((nw - 1,)),
            DMA((sources,)),
            DMA((tiles,)),
            DMA((tiles,)),
            DMA((tiles, nh - 1)),
            DMA((tiles, nh - 1)),
        ],
        compiler_params=pltpu.CompilerParams(
            collective_id=0, has_side_effects=True, vmem_limit_bytes=60 * 2**20
        ),
        cost_estimate=pl.CostEstimate(
            flops=4 * rows * features * columns,
            bytes_accessed=4 * features * columns,
            transcendentals=row_tp * columns,
        ),
    )(
        tokens,
        adapter_ids.reshape(1, row_dev),
        adapter_slot.reshape(1, -1),
        gate_weight,
        up_weight,
        hidden_unit_scales,
        shrink_weight,
        expand_weight,
    )


def solution(mesh):
    return jax.shard_map(
        functools.partial(shards, mesh.shape["wide"], mesh.shape["tp"]),
        mesh=mesh,
        in_specs=(
            P(("rep", "wide"), "tp"),
            P(("rep", "wide")),
            P(),
            P("tp", "wide"),
            P("tp", "wide"),
            P(None, "wide"),
            P("wide", "tp", None),
            P("tp", None, None, "wide"),
        ),
        out_specs=P(("rep", "tp"), "wide"),
        check_vma=False,
    )
```
